32 devices in a mesh: dp: 8 (over y, x, core), seq: 4 (over z).
Axes of the slice: x: 2, y: 2, z: 4, core: 2. Of those that a mesh axis runs over, the one named last changes fastest.
Arguments:
- queries: bfloat16 [8, 2048, 2048], P('dp', 'seq'), may hold values from -650 to 650
- keys_values: bfloat16 [8, 2048, 1024], P('dp', 'seq'), may hold values from -28 to 28
- doc_blocks: int32 [8, 16], P('dp'), may hold values from 0 to 3, never falling along the last dimension, each value on 1 to 8 neighbouring positions
- route_plan: int32 [4, 4], P('seq'), may hold values from 0 to 7, as said below
- out_weight: bfloat16 [2048, 4096], P('dp'), may hold values from -0.125 to 0.125
Outputs:
- layer_out: bfloat16 [8, 2048, 4096], P('dp', 'seq')
The draws below stay inside these ranges and needn't reach their ends.
Inputs may be any that keep to these rules, and one draw needn't show every extreme that they name: Within a row of route_plan the entries are distinct.
All inputs are finite; a program needn't handle non-finite values.
Results may differ from the reference program's by a relative error of at most 0.0053.
Values may be sent and summed in bfloat16 or wider, within the bound.
A program may use at most 256 MiB of HBM per device.

```python
import math
import jax
import jax.numpy as jnp
import numpy as np
from jax import lax

D = 4096
HEADS = 16
KV_HEADS = 4
HEAD_DIM = 128
BLOCK = 128
SEQ_LEN = 2048
NB = 16
NBD = 4
N_DP = 8
N_SEQ = 4


def draw_pairs_base(key):
    base = jax.random.normal(jax.random.fold_in(key, 11), (N_DP, SEQ_LEN, KV_HEADS, 2, HEAD_DIM), jnp.float32)
    return base


def draw_keys_values(key, part):
    base = draw_pairs_base(key)
    return base.reshape(N_DP, SEQ_LEN, KV_HEADS * 2 * HEAD_DIM).astype(jnp.bfloat16)


def draw_queries(key, part):
    grouped = HEADS // KV_HEADS
    base = jax.random.normal(jax.random.fold_in(key, 21), (N_DP, SEQ_LEN, KV_HEADS, grouped, HEAD_DIM), jnp.float32)
    return base.reshape(N_DP, SEQ_LEN, HEADS * HEAD_DIM).astype(jnp.bfloat16)


def permute_one(sub_key):
    return jax.random.permutation(sub_key, N_DP)


def draw_route_plan(key, part):
    sub_keys = jax.random.split(jax.random.fold_in(key, 31), N_SEQ)
    orders = jax.vmap(permute_one)(sub_keys)
    return orders[:, :NBD].astype(jnp.int32)


def levels(stream_key, shape, cuts, least, top_value):
    loudness = 1.0
    for dim, blocks in cuts:
        draws = jax.random.uniform(jax.random.fold_in(jax.random.fold_in(stream_key, 6), dim), (blocks,), jnp.float32, least / len(cuts), top_value / len(cuts))
        loudness = loudness * jnp.repeat(jnp.exp(draws), shape[dim] // blocks).reshape((-1,) + (1,) * (len(shape) - 1 - dim))
    return loudness


def split_up(amount, total, reach, slope):
    portions = [(1 << 20) // math.isqrt(grade ** slope) + 1 for grade in range(2, amount + 1)]
    spare, given = total - reach - (amount - 1), [1] * (amount - 1)
    while spare > 0:
        movable = [i for i in range(amount - 1) if given[i] < reach]
        mass, budget = sum([portions[i] for i in movable]), spare
        for i in movable:
            more = min(reach - given[i], max(1, budget * portions[i] // mass), spare)
            given[i] = given[i] + more
            spare = spare - more
    return np.array([reach] + given)


def uneven_parts(own_key, count, total, most, slope):
    if count == 2:
        one = jax.random.randint(own_key, (), max(1, total - most), min(most, total - 1) + 1)
        return jnp.stack([one, total - one])
    sizes = jnp.asarray(split_up(count, total, most, slope), jnp.int32)
    twos = (count - 1) // 2
    source_of, taker = sizes[1:1 + 2 * twos:2], sizes[2:2 + 2 * twos:2]
    room = jnp.minimum(source_of - 1, most - taker)
    moved = jax.random.randint(jax.random.fold_in(own_key, 1), (twos,), 0, 1 << 20) % (room + 1)
    sizes = sizes.at[1:1 + 2 * twos:2].set(source_of - moved).at[2:2 + 2 * twos:2].set(taker + moved)
    return sizes[jax.random.permutation(jax.random.fold_in(own_key, 2), count)]


def gaussian(stream_key, dims, deviation, bound, cuts=(), kind=jnp.bfloat16):
    loudness = levels(stream_key, dims, cuts, -0.22, 0.18) if cuts else 1.0
    values = jax.random.normal(stream_key, dims, jnp.float32) * deviation * loudness
    return jnp.minimum(jnp.maximum(values, -bound), bound).astype(kind)


def setup_inputs(seed: int = 0) -> dict:
    streams_of = jax.random.split(jax.random.key(seed), 6)
    return {
        "queries": draw_queries(jax.random.fold_in(streams_of[5], 71), 0),
        "keys_values": draw_keys_values(jax.random.fold_in(streams_of[5], 71), 0),
        "doc_blocks": jax.vmap(lambda own: jnp.searchsorted(jnp.cumsum(uneven_parts(own, max(3, NB // 4), NB, max(2, NB // 2), 2)), jnp.arange(NB), side="right"))(jax.random.split(streams_of[2], N_DP)).reshape((N_DP, NB)).astype(jnp.int32),
        "route_plan": draw_route_plan(jax.random.fold_in(streams_of[5], 71), 0),
        "out_weight": gaussian(streams_of[4], (HEADS * HEAD_DIM, D), (HEADS * HEAD_DIM) ** -0.5, 0.125, ((0, 8),)),
    }


neg_fill = -1e+30

def attend_group(query_rows, pair_rows, doc_ids):
    seq_rows = query_rows.shape[0]
    grouped = HEADS // KV_HEADS
    query_view = query_rows.reshape(seq_rows, KV_HEADS, grouped, HEAD_DIM).astype(jnp.float32)
    pair_view = pair_rows.reshape(seq_rows, KV_HEADS, 2, HEAD_DIM).astype(jnp.float32)
    key_view = pair_view[:, :, 0]
    value_view = pair_view[:, :, 1]
    token_doc = jnp.repeat(doc_ids, BLOCK)
    tile_rows = min(512, seq_rows)
    key_pos = jnp.arange(seq_rows, dtype=jnp.int32)
    score_scale = 1.0 / math.sqrt(HEAD_DIM)

    def per_tile(tile_index):
        first_row = tile_index * tile_rows
        query_tile = lax.dynamic_slice_in_dim(query_view, first_row, tile_rows, 0)
        query_pos = first_row + jnp.arange(tile_rows, dtype=jnp.int32)
        query_doc = lax.dynamic_slice_in_dim(token_doc, first_row, tile_rows, 0)
        scores = jnp.einsum('qcgd,kcd->cgqk', query_tile, key_view) * score_scale
        allowed = (query_doc[:, None] == token_doc[None, :]) & (key_pos[None, :] <= query_pos[:, None])
        scores = jnp.where(allowed, scores, neg_fill)
        row_max = scores.max(-1, keepdims=True)
        weights = jnp.where(allowed, jnp.exp(scores - row_max), 0.0)
        totals = weights.sum(-1)
        rounded = lax.optimization_barrier(weights.astype(jnp.bfloat16))
        mixed = jnp.einsum('cgqk,kcd->qcgd', rounded.astype(jnp.float32), value_view)
        attended = mixed / jnp.transpose(totals, (2, 0, 1))[..., None]
        return attended.astype(jnp.bfloat16).reshape(tile_rows, HEADS * HEAD_DIM)
    tile_out = lax.map(per_tile, jnp.arange(seq_rows // tile_rows, dtype=jnp.int32))
    return tile_out.reshape(seq_rows, HEADS * HEAD_DIM)

def reference(queries, keys_values, doc_blocks, route_plan, out_weight):
    flat_marks = route_plan.reshape(NB).astype(jnp.int32)
    groups = jnp.arange(N_DP, dtype=jnp.int32)[:, None]
    source = jnp.bitwise_xor(groups, flat_marks[None, :])
    places = jnp.broadcast_to(jnp.arange(NB, dtype=jnp.int32)[None, :], (N_DP, NB))
    moved_query = queries.reshape(N_DP, NB, BLOCK, HEADS * HEAD_DIM)[source, places]
    moved_query = moved_query.reshape(N_DP, SEQ_LEN, HEADS * HEAD_DIM)
    moved_pairs = keys_values.reshape(N_DP, NB, BLOCK, KV_HEADS * 2 * HEAD_DIM)[source, places]
    moved_pairs = moved_pairs.reshape(N_DP, SEQ_LEN, KV_HEADS * 2 * HEAD_DIM)

    def one_group(inputs):
        query_rows, pair_rows, doc_ids = inputs
        attended = attend_group(query_rows, pair_rows, doc_ids)
        return jnp.dot(attended, out_weight, preferred_element_type=jnp.float32).astype(jnp.bfloat16)
    return lax.map(one_group, (moved_query, moved_pairs, doc_blocks))
```

```python
import functools
import math

import jax
import jax.numpy as jnp
from jax import lax
from jax.experimental import pallas as pl
from jax.experimental.pallas import tpu as pltpu
from jax.sharding import PartitionSpec as P

HEAD_DIM = 128
BLOCK = 128
VARIANTS = 4


def attend_kernel(blocks, stride, group, table, q_ref, kv_ref, out_ref):
    pair = 2 if group % 2 == 0 else 1
    scale = math.log2(math.e) / math.sqrt(HEAD_DIM)

    def step(t, carry):
        i = t // (group // pair)
        h = t % (group // pair)
        place = table[0, i]
        count = table[1, i]
        variant = (count + stride - 1) // stride
        row = pl.multiple_of(i * BLOCK, BLOCK)
        col = pl.multiple_of(h * pair * HEAD_DIM, pair * HEAD_DIM)
        for v in range(1, VARIANTS + 1):

            @pl.when(variant == v)
            def _(v=v):
                n = v * stride
                first = pl.multiple_of((place - n + 1) * BLOCK, BLOCK)
                q = q_ref[pl.ds(row, BLOCK), pl.ds(col, pair * HEAD_DIM)]
                q = jnp.concatenate(
                    [q[:, a * HEAD_DIM : (a + 1) * HEAD_DIM] for a in range(pair)], axis=0
                )
                k = kv_ref[pl.ds(first, n * BLOCK), :HEAD_DIM]
                val = kv_ref[pl.ds(first, n * BLOCK), HEAD_DIM:]
                s = lax.dot_general(
                    q, k, (((1,), (1,)), ((), ())), preferred_element_type=jnp.float32
                )
                rows = pair * BLOCK
                lead = stride * BLOCK
                at = lax.broadcasted_iota(jnp.int32, (rows, n * BLOCK), 1)
                low = (n - count) * BLOCK
                high = (n - 1) * BLOCK + lax.rem(
                    lax.broadcasted_iota(jnp.int32, (rows, n * BLOCK), 0), BLOCK
                )
                parts = []
                for b in range(n):
                    sl = slice(b * BLOCK, (b + 1) * BLOCK)
                    piece = s[:, sl]
                    if b < stride - 1:
                        piece = jnp.where(at[:, sl] >= low, piece, -jnp.inf)
                    if b == n - 1:
                        piece = jnp.where(at[:, sl] <= high[:, sl], piece, -jnp.inf)
                    parts.append(piece)
                top = functools.reduce(jnp.maximum, parts)
                top = jnp.max(top, axis=1, keepdims=True)
                w = jnp.concatenate(
                    [jnp.exp2((piece - top) * scale).astype(jnp.bfloat16) for piece in parts],
                    axis=1,
                )
                ext = jnp.concatenate([val, jnp.ones_like(val)], axis=1)
                mixed = jnp.dot(w, ext, preferred_element_type=jnp.float32)
                att = (mixed[:, :HEAD_DIM] / mixed[:, HEAD_DIM:]).astype(jnp.bfloat16)
                out_ref[pl.ds(row, BLOCK), pl.ds(col, pair * HEAD_DIM)] = jnp.concatenate(
                    [att[a * BLOCK : (a + 1) * BLOCK] for a in range(pair)], axis=1
                )

        return carry

    lax.fori_loop(0, blocks * (group // pair), step, 0)


def attend(queries, context, table, stride):
    rows, width = queries.shape
    pairs = context.shape[1] // (2 * HEAD_DIM)
    group = width // HEAD_DIM // pairs
    blocks = rows // BLOCK
    return pl.pallas_call(
        functools.partial(attend_kernel, blocks, stride, group),
        grid_spec=pltpu.PrefetchScalarGridSpec(
            num_scalar_prefetch=1,
            grid=(pairs,),
            in_specs=[
                pl.BlockSpec((rows, group * HEAD_DIM), lambda c, t: (0, c)),
                pl.BlockSpec((context.shape[0], 2 * HEAD_DIM), lambda c, t: (0, c)),
            ],
            out_specs=pl.BlockSpec((rows, group * HEAD_DIM), lambda c, t: (0, c)),
        ),
        out_shape=jax.ShapeDtypeStruct((rows, width), jnp.bfloat16),
        compiler_params=pltpu.CompilerParams(vmem_limit_bytes=40 * 1024 * 1024),
        cost_estimate=pl.CostEstimate(
            flops=10**10, bytes_accessed=8 * 10**6, transcendentals=10**6
        ),
        name="attend",
    )(table, queries, context)


def swap_bit(block, marks, bit):
    count = lax.axis_size("dp")
    route = [(g, g ^ (1 << bit)) for g in range(count)]
    partner = lax.ppermute(block, "dp", route)
    moving = (jnp.right_shift(marks, bit) % 2 == 1)[:, None, None]
    return jnp.where(moving, partner, block)


def exchange(block, marks):
    half = block.shape[2] // 2
    bits = list(range(lax.axis_size("dp").bit_length() - 1))
    done = []
    for part, order in ((block[:, :, :half], bits), (block[:, :, half:], bits[:1] + bits[:0:-1])):
        for bit in order:
            part = swap_bit(part, marks, bit)
        done.append(part)
    return jnp.concatenate(done, axis=2)


def body(queries, keys_values, doc_blocks, route_plan, out_weight):
    rows = queries.shape[1]
    blocks = rows // BLOCK
    seq_count = lax.axis_size("seq")
    total_blocks = doc_blocks.shape[1]
    longest = total_blocks // 2
    hops = (longest - 1 + blocks - 1) // blocks
    stride = max(1, longest // VARIANTS)
    marks = route_plan[0]
    own_pairs = exchange(keys_values[0].reshape(blocks, BLOCK, -1), marks).reshape(rows, -1)
    own_queries = exchange(queries[0].reshape(blocks, BLOCK, -1), marks).reshape(rows, -1)
    ring = [(s, s + 1) for s in range(seq_count - 1)]
    context = [own_pairs]
    for _ in range(hops):
        context.insert(0, lax.ppermute(context[0], "seq", ring))
    context = jnp.concatenate(context, axis=0)
    docs = doc_blocks[0]
    own = lax.axis_index("seq") * blocks + jnp.arange(blocks, dtype=jnp.int32)
    own_docs = docs[own]
    start = jnp.sum((docs[None, :] < own_docs[:, None]).astype(jnp.int32), axis=1)
    place = hops * blocks + jnp.arange(blocks, dtype=jnp.int32)
    table = jnp.stack([place, own - start + 1])
    attended = attend(own_queries, context, table, stride)
    layer_out = jnp.dot(
        attended,
        lax.all_gather(out_weight, "dp", axis=0, tiled=True),
        preferred_element_type=jnp.float32,
    )
    return layer_out.astype(jnp.bfloat16)[None]


def solution(mesh):
    in_specs = (
        P("dp", "seq", None),
        P("dp", "seq", None),
        P("dp", None),
        P("seq", None),
        P("dp", None),
    )
    out_specs = P("dp", "seq", None)
    return jax.shard_map(body, mesh=mesh, in_specs=in_specs, out_specs=out_specs, check_vma=False)
```

```python
import functools
import math

import jax
import jax.numpy as jnp
from jax import lax
from jax.experimental import pallas as pl
from jax.experimental.pallas import tpu as pltpu
from jax.sharding import PartitionSpec as P

HEAD_DIM = 128
BLOCK = 128
MESH = pl.DeviceIdType.MESH


def layer_kernel(
    groups,
    seq_count,
    longest,
    hops,
    doc_ref,
    route_ref,
    q_ref,
    kv_ref,
    w_ref,
    out_ref,
    full_ref,
    q_out,
    q_in,
    kv_out,
    kv_in,
    ctx,
    q_send,
    q_recv,
    kv_send,
    kv_recv,
    w_send,
    w_recv,
    hop_send,
    hop_recv,
    own_sem,
):
    me = lax.axis_index("dp")
    s = lax.axis_index("seq")
    blocks = q_ref.shape[0]
    n_docs = doc_ref.shape[1]
    bit_count = groups.bit_length() - 1
    place = hops * blocks
    bit_of = [lax.rem(lax.div(me, 1 << b), 2) for b in range(bit_count)]

    def partner(offset):
        at = me
        for b in range(bit_count):
            if offset >> b & 1:
                at = at + (1 - 2 * bit_of[b]) * (1 << b)
        return at

    peers = [partner(d) for d in range(groups)]
    right = lax.rem(s + 1, seq_count)
    left = lax.rem(s + seq_count - 1, seq_count)

    barrier = pltpu.get_barrier_semaphore()
    for d in range(1, groups):
        pl.semaphore_signal(barrier, inc=1, device_id={"dp": peers[d]}, device_id_type=MESH)
    for side in (left, right):
        pl.semaphore_signal(barrier, inc=1, device_id={"seq": side}, device_id_type=MESH)

    marks = [route_ref[0, j] for j in range(blocks)]
    taken = []
    for d in range(groups):
        at = jnp.int32(0)
        for j in range(1, blocks):
            at = jnp.where(marks[j] == d, j, at)
        taken.append(at)
    for d in range(1, groups):
        kv_out[d] = kv_ref[taken[d]]
    kv_in[0] = kv_ref[taken[0]]
    pl.semaphore_wait(barrier, groups + 1)

    def slot_copy(src, dst, send, recv, d):
        return pltpu.make_async_remote_copy(
            src_ref=src.at[d],
            dst_ref=dst.at[d],
            send_sem=send.at[d],
            recv_sem=recv.at[d],
            device_id={"dp": peers[d]},
            device_id_type=MESH,
        )

    order = list(range(groups - 1, 0, -1))
    kv_copies = [slot_copy(kv_out, kv_in, kv_send, kv_recv, d) for d in order]
    q_copies = [slot_copy(q_out, q_in, q_send, q_recv, d) for d in order]
    for copy in kv_copies:
        copy.start()
    for d in range(1, groups):
        q_out[d] = q_ref[taken[d]]
    q_in[0] = q_ref[taken[0]]
    for copy in kv_copies:
        copy.wait_send()
    for copy in q_copies:
        copy.start()
    for copy in kv_copies:
        copy.wait_recv()
    for j in range(blocks):
        ctx[pl.ds((place + j) * BLOCK, BLOCK), :] = kv_in[marks[j]]

    for h in range(1, hops + 1):
        skip = place - longest + 1 if h == hops else 0
        rows = (blocks - skip) * BLOCK
        to = ((hops - h) * blocks + skip) * BLOCK
        copy = pltpu.make_async_remote_copy(
            src_ref=ctx.at[pl.ds(to + blocks * BLOCK, rows)],
            dst_ref=ctx.at[pl.ds(to, rows)],
            send_sem=hop_send.at[h - 1],
            recv_sem=hop_recv.at[h - 1],
            device_id={"seq": right},
            device_id_type=MESH,
        )

        @pl.when((s >= h - 1) & (s < seq_count - 1))
        def _(copy=copy):
            copy.start()

        @pl.when(s < h)
        def _(to=to, rows=rows):
            ctx[pl.ds(to, rows), :] = jnp.zeros((rows, ctx.shape[1]), ctx.dtype)

        @pl.when(s >= h)
        def _(copy=copy):
            copy.wait_recv()

        @pl.when((s >= h - 1) & (s < seq_count - 1))
        def _(copy=copy):
            copy.wait_send()

    shard = w_ref.shape[0]
    half_rows = shard // 2
    chip_bits = list(range(1, bit_count))
    paths = (chip_bits, chip_bits[::-1])

    def rows_of(half, offset):
        return pl.ds(pl.multiple_of(peers[offset] * shard + half * half_rows, half_rows), half_rows)

    def piece_copy(half, phase, offset, bit):
        source = w_ref.at[pl.ds(half * half_rows, half_rows)] if offset == 0 else full_ref.at[rows_of(half, offset)]
        return pltpu.make_async_remote_copy(
            src_ref=source,
            dst_ref=full_ref.at[rows_of(half, offset)],
            send_sem=w_send.at[half, phase, offset],
            recv_sem=w_recv.at[half, offset ^ (1 << bit)],
            device_id={"dp": peers[1 << bit]},
            device_id_type=MESH,
        )

    def arrived(half, offset):
        pltpu.make_async_remote_copy(
            src_ref=full_ref.at[rows_of(half, offset)],
            dst_ref=full_ref.at[rows_of(half, offset)],
            send_sem=w_send.at[half, 0, 0],
            recv_sem=w_recv.at[half, offset],
            device_id={"dp": peers[1]},
            device_id_type=MESH,
        ).wait_recv()

    for copy in q_copies[:-2]:
        copy.wait_send()
    sent = []
    own = pltpu.make_async_copy(
        w_ref, full_ref.at[pl.ds(pl.multiple_of(me * shard, shard), shard)], own_sem
    )
    for phase in range(len(chip_bits)):
        for half in range(2):
            sent.append(piece_copy(half, phase, 0, paths[half][phase]))
            sent[-1].start()
    own.start()
    for half in range(2):
        sent.append(piece_copy(half, bit_count - 1, 0, 0))
        sent[-1].start()
    for copy in q_copies[-2:]:
        copy.wait_send()
    for copy in q_copies:
        copy.wait_recv()

    pairs = kv_ref.shape[2] // (2 * HEAD_DIM)
    group = q_ref.shape[2] // HEAD_DIM // pairs
    wide = 2 if group % 2 == 0 else 1
    scale = math.log2(math.e) / math.sqrt(HEAD_DIM)
    per_pair = group // wide

    def attend(t, carry):
        i = lax.div(t, pairs * per_pair)
        u = lax.rem(t, pairs * per_pair)
        c = lax.div(u, per_pair)
        mine = s * blocks + i
        doc = doc_ref[0, mine]
        start = jnp.int32(0)
        for b in range(n_docs):
            start = start + jnp.where(doc_ref[0, b] < doc, 1, 0)
        low = (longest - 1 - mine + start) * BLOCK
        col = pl.multiple_of(u * wide * HEAD_DIM, wide * HEAD_DIM)
        q = q_in[route_ref[0, i], :, pl.ds(col, wide * HEAD_DIM)]
        q = jnp.concatenate(
            [q[:, a * HEAD_DIM : (a + 1) * HEAD_DIM] for a in range(wide)], axis=0
        )
        first = pl.multiple_of((place + 1 - longest + i) * BLOCK, BLOCK)
        kcol = pl.multiple_of(c * 2 * HEAD_DIM, 2 * HEAD_DIM)
        window = ctx[pl.ds(first, longest * BLOCK), pl.ds(kcol, 2 * HEAD_DIM)]
        k = window[:, :HEAD_DIM]
        val = window[:, HEAD_DIM:]
        scores = lax.dot_general(
            q, k, (((1,), (1,)), ((), ())), preferred_element_type=jnp.float32
        )
        rows = wide * BLOCK
        column = lax.broadcasted_iota(jnp.int32, (rows, BLOCK), 1)
        row = lax.rem(lax.broadcasted_iota(jnp.int32, (rows, BLOCK), 0), BLOCK)
        parts = []
        for b in range(longest):
            piece = scores[:, b * BLOCK : (b + 1) * BLOCK]
            if b < longest - 1:
                piece = jnp.where(column >= low - b * BLOCK, piece, -jnp.inf)
            else:
                piece = jnp.where(column <= row, piece, -jnp.inf)
            parts.append(piece)
        top = jnp.max(functools.reduce(jnp.maximum, parts), axis=1, keepdims=True)
        weights = jnp.concatenate(
            [jnp.exp2((piece - top) * scale).astype(jnp.bfloat16) for piece in parts], axis=1
        )
        mixed = jnp.dot(
            weights,
            jnp.concatenate([val, jnp.ones_like(val)], axis=1),
            preferred_element_type=jnp.float32,
        )
        att = (mixed[:, :HEAD_DIM] / mixed[:, HEAD_DIM:]).astype(jnp.bfloat16)
        out_ref[pl.ds(pl.multiple_of(i * BLOCK, BLOCK), BLOCK), pl.ds(col, wide * HEAD_DIM)] = (
            jnp.concatenate([att[a * BLOCK : (a + 1) * BLOCK] for a in range(wide)], axis=1)
        )
        return carry

    lax.fori_loop(0, blocks * pairs * per_pair, attend, 0)

    seen = set()

    def need(half, offset):
        if (half, offset) not in seen:
            seen.add((half, offset))
            arrived(half, offset)

    held = [[0], [0]]
    for phase in range(len(chip_bits)):
        for half in range(2):
            bit = paths[half][phase]
            for offset in held[half]:
                if offset:
                    need(half, offset)
                    sent.append(piece_copy(half, phase, offset, bit))
                    sent[-1].start()
            held[half] = held[half] + [o ^ (1 << bit) for o in held[half]]
    for place_in in range(1, len(held[0])):
        for half in range(2):
            offset = held[half][place_in]
            need(half, offset)
            sent.append(piece_copy(half, bit_count - 1, offset, 0))
            sent[-1].start()
    for half in range(2):
        for offset in range(1, groups, 2):
            need(half, offset)
    own.wait()
    for copy in sent:
        copy.wait_send()


def body(queries, keys_values, doc_blocks, route_plan, out_weight):
    rows, width = queries.shape[1:]
    pair_width = keys_values.shape[2]
    blocks = rows // BLOCK
    seq_count = lax.axis_size("seq")
    groups = lax.axis_size("dp")
    bit_count = groups.bit_length() - 1
    longest = doc_blocks.shape[1] // 2
    hops = (longest - 1 + blocks - 1) // blocks
    dtype = queries.dtype
    vmem = pl.BlockSpec(memory_space=pltpu.VMEM)
    smem = pl.BlockSpec(memory_space=pltpu.SMEM)
    anyspace = pl.BlockSpec(memory_space=pl.ANY)
    dma = pltpu.SemaphoreType.DMA
    attended, weight = pl.pallas_call(
        functools.partial(layer_kernel, groups, seq_count, longest, hops),
        in_specs=[smem, smem, vmem, vmem, anyspace],
        out_specs=[vmem, anyspace],
        out_shape=[
            jax.ShapeDtypeStruct((rows, width), dtype),
            jax.ShapeDtypeStruct((out_weight.shape[0] * groups, out_weight.shape[1]), dtype),
        ],
        scratch_shapes=[
            pltpu.VMEM((groups, BLOCK, width), dtype),
            pltpu.VMEM((groups, BLOCK, width), dtype),
            pltpu.VMEM((groups, BLOCK, pair_width), dtype),
            pltpu.VMEM((groups, BLOCK, pair_width), dtype),
            pltpu.VMEM(((hops + 1) * rows, pair_width), dtype),
            dma((groups,)),
            dma((groups,)),
            dma((groups,)),
            dma((groups,)),
            dma((2, bit_count, groups)),
            dma((2, groups)),
            dma((hops,)),
            dma((hops,)),
            dma,
        ],
        compiler_params=pltpu.CompilerParams(
            collective_id=0, has_side_effects=True, vmem_limit_bytes=52 * 1024 * 1024
        ),
        cost_estimate=pl.CostEstimate(
            flops=10**10, bytes_accessed=3 * 10**7, transcendentals=10**7
        ),
        name="layer",
    )(
        doc_blocks,
        route_plan,
        queries[0].reshape(blocks, BLOCK, width),
        keys_values[0].reshape(blocks, BLOCK, pair_width),
        out_weight,
    )
    layer_out = jnp.dot(attended, weight, preferred_element_type=jnp.float32)
    return layer_out.astype(jnp.bfloat16)[None]


def solution(mesh):
    in_specs = (
        P("dp", "seq", None),
        P("dp", "seq", None),
        P("dp", None),
        P("seq", None),
        P("dp", None),
    )
    out_specs = P("dp", "seq", None)
    return jax.shard_map(body, mesh=mesh, in_specs=in_specs, out_specs=out_specs, check_vma=False)
```

```python
import functools
import math

import jax
import jax.numpy as jnp
from jax import lax
from jax.experimental import pallas as pl
from jax.experimental.pallas import tpu as pltpu
from jax.sharding import PartitionSpec as P

HEAD_DIM = 128
BLOCK = 128
PARTS = 4
MESH = pl.DeviceIdType.MESH


def layer_kernel(
    groups,
    seq_count,
    longest,
    hops,
    doc_ref,
    route_ref,
    q_ref,
    kv_ref,
    w_ref,
    out_ref,
    full_ref,
    q_out,
    q_in,
    kv_out,
    kv_in,
    ctx,
    q_send,
    q_recv,
    kv_send,
    kv_recv,
    w_send,
    w_recv,
    hop_send,
    hop_recv,
    own_sem,
):
    me = lax.axis_index("dp")
    s = lax.axis_index("seq")
    blocks = q_ref.shape[0]
    n_docs = doc_ref.shape[1]
    bit_count = groups.bit_length() - 1
    place = hops * blocks
    bit_of = [lax.rem(lax.div(me, 1 << b), 2) for b in range(bit_count)]

    def partner(offset):
        at = me
        for b in range(bit_count):
            if offset >> b & 1:
                at = at + (1 - 2 * bit_of[b]) * (1 << b)
        return at

    peers = [partner(d) for d in range(groups)]
    right = lax.rem(s + 1, seq_count)
    left = lax.rem(s + seq_count - 1, seq_count)

    barrier = pltpu.get_barrier_semaphore()
    for d in range(1, groups):
        pl.semaphore_signal(barrier, inc=1, device_id={"dp": peers[d]}, device_id_type=MESH)
    for side in (left, right):
        pl.semaphore_signal(barrier, inc=1, device_id={"seq": side}, device_id_type=MESH)

    marks = [route_ref[0, j] for j in range(blocks)]
    taken = []
    for d in range(groups):
        at = jnp.int32(0)
        for j in range(1, blocks):
            at = jnp.where(marks[j] == d, j, at)
        taken.append(at)
    for d in range(1, groups):
        kv_out[d] = kv_ref[taken[d]]
    kv_in[0] = kv_ref[taken[0]]
    pl.semaphore_wait(barrier, groups + 1)

    def slot_copy(src, dst, send, recv, d):
        return pltpu.make_async_remote_copy(
            src_ref=src.at[d],
            dst_ref=dst.at[d],
            send_sem=send.at[d],
            recv_sem=recv.at[d],
            device_id={"dp": peers[d]},
            device_id_type=MESH,
        )

    order = list(range(groups - 1, 0, -1))
    kv_copies = [slot_copy(kv_out, kv_in, kv_send, kv_recv, d) for d in order]
    q_copies = [slot_copy(q_out, q_in, q_send, q_recv, d) for d in order]
    for copy in kv_copies:
        copy.start()
    for d in range(1, groups):
        q_out[d] = q_ref[taken[d]]
    q_in[0] = q_ref[taken[0]]
    for at, copy in enumerate(q_copies):
        kv_copies[at].wait_send()
        copy.start()
    for copy in kv_copies:
        copy.wait_recv()
    for j in range(blocks):
        ctx[pl.ds((place + j) * BLOCK, BLOCK), :] = kv_in[marks[j]]

    shard = w_ref.shape[0]
    half_rows = shard // PARTS
    chip_bits = list(range(1, bit_count))
    paths = [chip_bits, chip_bits[::-1]] * (PARTS // 2)

    def rows_of(half, offset):
        return pl.ds(pl.multiple_of(peers[offset] * shard + half * half_rows, half_rows), half_rows)

    def piece_copy(half, phase, offset, bit):
        source = w_ref.at[pl.ds(half * half_rows, half_rows)] if offset == 0 else full_ref.at[rows_of(half, offset)]
        return pltpu.make_async_remote_copy(
            src_ref=source,
            dst_ref=full_ref.at[rows_of(half, offset)],
            send_sem=w_send.at[half, phase, offset],
            recv_sem=w_recv.at[half, offset ^ (1 << bit)],
            device_id={"dp": peers[1 << bit]},
            device_id_type=MESH,
        )

    def arrived(half, offset):
        pltpu.make_async_remote_copy(
            src_ref=full_ref.at[rows_of(half, offset)],
            dst_ref=full_ref.at[rows_of(half, offset)],
            send_sem=w_send.at[half, 0, 0],
            recv_sem=w_recv.at[half, offset],
            device_id={"dp": peers[1]},
            device_id_type=MESH,
        ).wait_recv()

    for h in range(1, hops + 1):
        skip = place - longest + 1 if h == hops else 0
        rows = (blocks - skip) * BLOCK
        to = ((hops - h) * blocks + skip) * BLOCK
        copy = pltpu.make_async_remote_copy(
            src_ref=ctx.at[pl.ds(to + blocks * BLOCK, rows)],
            dst_ref=ctx.at[pl.ds(to, rows)],
            send_sem=hop_send.at[h - 1],
            recv_sem=hop_recv.at[h - 1],
            device_id={"seq": right},
            device_id_type=MESH,
        )

        @pl.when((s >= h - 1) & (s < seq_count - 1))
        def _(copy=copy):
            copy.start()

        @pl.when(s < h)
        def _(to=to, rows=rows):
            ctx[pl.ds(to, rows), :] = jnp.zeros((rows, ctx.shape[1]), ctx.dtype)

        if h == hops:
            for first_copy in q_copies[:-2]:
                first_copy.wait_send()
            sent = []
            own = pltpu.make_async_copy(
                w_ref, full_ref.at[pl.ds(pl.multiple_of(me * shard, shard), shard)], own_sem
            )
            for phase in range(len(chip_bits)):
                for half in range(PARTS):
                    sent.append(piece_copy(half, phase, 0, paths[half][phase]))
                    sent[-1].start()
            own.start()
            for half in range(PARTS):
                sent.append(piece_copy(half, bit_count - 1, 0, 0))
                sent[-1].start()

        @pl.when(s >= h)
        def _(copy=copy):
            copy.wait_recv()

        @pl.when((s >= h - 1) & (s < seq_count - 1))
        def _(copy=copy):
            copy.wait_send()

    for copy in q_copies[-2:]:
        copy.wait_send()
    for copy in q_copies:
        copy.wait_recv()

    pairs = kv_ref.shape[2] // (2 * HEAD_DIM)
    group = q_ref.shape[2] // HEAD_DIM // pairs
    wide = 2 if group % 2 == 0 else 1
    scale = math.log2(math.e) / math.sqrt(HEAD_DIM)
    per_pair = group // wide

    def attend(t, carry):
        i = lax.div(t, pairs * per_pair)
        u = lax.rem(t, pairs * per_pair)
        c = lax.div(u, per_pair)
        mine = s * blocks + i
        doc = doc_ref[0, mine]
        start = jnp.int32(0)
        for b in range(n_docs):
            start = start + jnp.where(doc_ref[0, b] < doc, 1, 0)
        low = (longest - 1 - mine + start) * BLOCK
        col = pl.multiple_of(u * wide * HEAD_DIM, wide * HEAD_DIM)
        q = q_in[route_ref[0, i], :, pl.ds(col, wide * HEAD_DIM)]
        q = jnp.concatenate(
            [q[:, a * HEAD_DIM : (a + 1) * HEAD_DIM] for a in range(wide)], axis=0
        )
        first = pl.multiple_of((place + 1 - longest + i) * BLOCK, BLOCK)
        kcol = pl.multiple_of(c * 2 * HEAD_DIM, 2 * HEAD_DIM)
        window = ctx[pl.ds(first, longest * BLOCK), pl.ds(kcol, 2 * HEAD_DIM)]
        k = window[:, :HEAD_DIM]
        val = window[:, HEAD_DIM:]
        scores = lax.dot_general(
            q, k, (((1,), (1,)), ((), ())), preferred_element_type=jnp.float32
        )
        rows = wide * BLOCK
        column = lax.broadcasted_iota(jnp.int32, (rows, BLOCK), 1)
        row = lax.rem(lax.broadcasted_iota(jnp.int32, (rows, BLOCK), 0), BLOCK)
        parts = []
        for b in range(longest):
            piece = scores[:, b * BLOCK : (b + 1) * BLOCK]
            if b < longest - 1:
                piece = jnp.where(column >= low - b * BLOCK, piece, -jnp.inf)
            else:
                piece = jnp.where(column <= row, piece, -jnp.inf)
            parts.append(piece)
        top = jnp.max(functools.reduce(jnp.maximum, parts), axis=1, keepdims=True)
        weights = jnp.concatenate(
            [jnp.exp2((piece - top) * scale).astype(jnp.bfloat16) for piece in parts], axis=1
        )
        mixed = jnp.dot(
            weights,
            jnp.concatenate([val, jnp.ones_like(val)], axis=1),
            preferred_element_type=jnp.float32,
        )
        att = (mixed[:, :HEAD_DIM] / mixed[:, HEAD_DIM:]).astype(jnp.bfloat16)
        out_ref[pl.ds(pl.multiple_of(i * BLOCK, BLOCK), BLOCK), pl.ds(col, wide * HEAD_DIM)] = (
            jnp.concatenate([att[a * BLOCK : (a + 1) * BLOCK] for a in range(wide)], axis=1)
        )
        return carry

    steps = blocks * pairs * per_pair
    lax.fori_loop(0, steps // 2, attend, 0)

    seen = set()

    def need(half, offset):
        if (half, offset) not in seen:
            seen.add((half, offset))
            arrived(half, offset)

    held = [[0] for _ in range(PARTS)]
    for phase in range(len(chip_bits)):
        for half in range(PARTS):
            bit = paths[half][phase]
            for offset in held[half]:
                if offset:
                    need(half, offset)
                    sent.append(piece_copy(half, phase, offset, bit))
                    sent[-1].start()
            held[half] = held[half] + [o ^ (1 << bit) for o in held[half]]
    lax.fori_loop(steps // 2, steps, attend, 0)
    for place_in in range(1, len(held[0])):
        for half in range(PARTS):
            offset = held[half][place_in]
            need(half, offset)
            sent.append(piece_copy(half, bit_count - 1, offset, 0))
            sent[-1].start()
    for half in range(PARTS):
        for offset in range(1, groups, 2):
            need(half, offset)
    own.wait()
    for copy in sent:
        copy.wait_send()


def body(queries, keys_values, doc_blocks, route_plan, out_weight):
    rows, width = queries.shape[1:]
    pair_width = keys_values.shape[2]
    blocks = rows // BLOCK
    seq_count = lax.axis_size("seq")
    groups = lax.axis_size("dp")
    bit_count = groups.bit_length() - 1
    longest = doc_blocks.shape[1] // 2
    hops = (longest - 1 + blocks - 1) // blocks
    dtype = queries.dtype
    vmem = pl.BlockSpec(memory_space=pltpu.VMEM)
    smem = pl.BlockSpec(memory_space=pltpu.SMEM)
    anyspace = pl.BlockSpec(memory_space=pl.ANY)
    dma = pltpu.SemaphoreType.DMA
    attended, weight = pl.pallas_call(
        functools.partial(layer_kernel, groups, seq_count, longest, hops),
        in_specs=[smem, smem, vmem, vmem, anyspace],
        out_specs=[vmem, anyspace],
        out_shape=[
            jax.ShapeDtypeStruct((rows, width), dtype),
            jax.ShapeDtypeStruct((out_weight.shape[0] * groups, out_weight.shape[1]), dtype),
        ],
        scratch_shapes=[
            pltpu.VMEM((groups, BLOCK, width), dtype),
            pltpu.VMEM((groups, BLOCK, width), dtype),
            pltpu.VMEM((groups, BLOCK, pair_width), dtype),
            pltpu.VMEM((groups, BLOCK, pair_width), dtype),
            pltpu.VMEM(((hops + 1) * rows, pair_width), dtype),
            dma((groups,)),
            dma((groups,)),
            dma((groups,)),
            dma((groups,)),
            dma((PARTS, bit_count, groups)),
            dma((PARTS, groups)),
            dma((hops,)),
            dma((hops,)),
            dma,
        ],
        compiler_params=pltpu.CompilerParams(
            collective_id=0, has_side_effects=True, vmem_limit_bytes=52 * 1024 * 1024
        ),
        cost_estimate=pl.CostEstimate(
            flops=10**10, bytes_accessed=3 * 10**7, transcendentals=10**7
        ),
        name="layer",
    )(
        doc_blocks,
        route_plan,
        queries[0].reshape(blocks, BLOCK, width),
        keys_values[0].reshape(blocks, BLOCK, pair_width),
        out_weight,
    )
    layer_out = jnp.dot(attended, weight, preferred_element_type=jnp.float32)
    return layer_out.astype(jnp.bfloat16)[None]


def solution(mesh):
    in_specs = (
        P("dp", "seq", None),
        P("dp", "seq", None),
        P("dp", None),
        P("seq", None),
        P("dp", None),
    )
    out_specs = P("dp", "seq", None)
    return jax.shard_map(body, mesh=mesh, in_specs=in_specs, out_specs=out_specs, check_vma=False)
```
